32 devices in a mesh: row: 4 (over z), col: 8 (over y, x, core).
Axes of the slice: x: 2, y: 2, z: 4, core: 2. Of those that a mesh axis runs over, the one named last changes fastest.
Arguments:
- src_emb: bfloat16 [32768, 256], P(('row', 'col')), may hold values from -64 to 64
- dst_emb: bfloat16 [32768, 256], P('col'), may hold values from -64 to 64
- state_emb: bfloat16 [32768, 256], P('col'), may hold values from -64 to 64
- word_emb: bfloat16 [32000, 256], P('row'), may hold values from -64 to 64
- start_probs: bfloat16 [64, 32768], P(None, 'row'), may hold values from 0.099609375 to 10
- token_ids: int32 [64, 2], replicated, may hold values from 0 to 31999
Outputs:
- final_probs: float32 [64, 32768], P(None, 'col')
- log_norm: float32 [64], replicated
The draws below stay inside these ranges and needn't reach their ends.
All inputs are finite; a program needn't handle non-finite values.
Results may differ from the reference program's by a relative error of at most 0.0003.
The reference program's roundings to bfloat16 on the way count: a program that leaves them out, or rounds other values in their place, can miss the bound.
Values may be sent and summed in bfloat16 or wider, within the bound.
No kernel may reach another device: no remote copies, remote signals or barrier semaphores. Data moves between devices by JAX's collectives and lax.ppermute only.
A program may use at most 256 MiB of HBM per device.

```python
import math
import jax
import jax.numpy as jnp
import numpy as np
from jax import lax

S = 32768
E = 256
V = 32000
B = 64
STEPS = 2


def drawn_pair(key, first_rows, second_rows):
    keys = jax.random.split(key, 2)
    spread = (3.0 / math.sqrt(E)) ** 0.5
    first = jnp.clip(jax.random.normal(keys[0], (first_rows, E), jnp.float32), -5.0, 5.0) * spread
    second = jnp.clip(jax.random.normal(keys[1], (second_rows, E), jnp.float32), -5.0, 5.0) * spread
    return (first, second)


def draw_src_emb(key, part):
    return drawn_pair(jax.random.fold_in(key, 11), S, S)[0].astype(jnp.bfloat16)


def draw_dst_emb(key, part):
    return drawn_pair(jax.random.fold_in(key, 11), S, S)[1].astype(jnp.bfloat16)


def draw_state_emb(key, part):
    return drawn_pair(jax.random.fold_in(key, 23), S, V)[0].astype(jnp.bfloat16)


def draw_word_emb(key, part):
    return drawn_pair(jax.random.fold_in(key, 23), S, V)[1].astype(jnp.bfloat16)


def plant(array, stream_key, low, high):
    extent = array.shape
    index_at = [jax.random.randint(jax.random.fold_in(stream_key, axis), (), 0, extent[axis]) for axis in range(len(extent))]
    array = array.at[tuple(index_at)].set(low)
    longest = extent.index(max(extent))
    index_at[longest] = (index_at[longest] + 1) % extent[longest]
    return array.at[tuple(index_at)].set(high)


def steps_of(key, extent, cuts, smallest, top_value):
    def one(axis_at, parts):
        steps = jax.random.uniform(jax.random.fold_in(jax.random.fold_in(key, 6), axis_at), (parts,), jnp.float32, smallest / len(cuts), top_value / len(cuts))
        return jnp.repeat(jnp.exp(steps), extent[axis_at] // parts).reshape((-1,) + (1,) * (len(extent) - axis_at - 1))

    gain = one(*cuts[0])
    for cut in cuts[1:]:
        gain = gain * one(*cut)
    return gain


def cumulative_ranks(count, slope):
    loads = [(1 << 20) // math.isqrt(rank ** slope) + 1 for rank in range(1, count + 1)]
    width = 1 + sum(loads) // (1 << 30)
    return np.cumsum(np.array([max(1, weight // width) for weight in loads]))


def skewed_ids(stream_key, shape, amount, skew):
    listing = cumulative_ranks(amount, skew)
    pick = jax.random.randint(jax.random.fold_in(stream_key, 1), shape, 0, int(listing[amount - 1]))
    standing = jnp.searchsorted(jnp.asarray(listing, jnp.int32), pick, side="right")
    return jax.random.permutation(jax.random.fold_in(stream_key, 2), amount)[standing].astype(jnp.int32)


def setup_inputs(seed: int = 0) -> dict:
    key_of = jax.random.split(jax.random.key(seed), 7)
    src_emb = draw_src_emb(jax.random.fold_in(key_of[6], 71), 0)
    dst_emb = draw_dst_emb(jax.random.fold_in(key_of[6], 71), 0)
    state_emb = draw_state_emb(jax.random.fold_in(key_of[6], 71), 0)
    word_emb = draw_word_emb(jax.random.fold_in(key_of[6], 71), 0)
    start_probs = jnp.clip(jnp.exp(math.log(10.0) - 4.609084 * jax.random.uniform(key_of[4], (B, S), jnp.float32) ** steps_of(key_of[4], (B, S), ((1, 4),), -0.2, 0.2)), 0.099609375, 10.0).astype(jnp.bfloat16)
    token_ids = plant(skewed_ids(key_of[5], (B, STEPS), V, 2), jax.random.fold_in(key_of[5], 3), 0, V - 1).astype(jnp.int32)
    return dict(src_emb=src_emb, dst_emb=dst_emb, state_emb=state_emb, word_emb=word_emb, start_probs=start_probs, token_ids=token_ids)


def reference(src_emb, dst_emb, state_emb, word_emb, start_probs, token_ids):
    block_rows = math.gcd(S, 1024)
    block_count = S // block_rows

    def vocab_block(rows):
        logits = jnp.dot(rows, word_emb.T, preferred_element_type=jnp.float32)
        top = jnp.max(logits, axis=1)
        return top + jnp.log(jnp.sum(jnp.exp(logits - top[:, None]), axis=1))

    state_norm = lax.map(vocab_block, state_emb.reshape(block_count, block_rows, E)).reshape(S)
    token_vecs = word_emb[token_ids.reshape(-1)]
    scores = jnp.dot(token_vecs, state_emb.T, preferred_element_type=jnp.float32)
    emit = jnp.exp(scores - state_norm[None, :]).reshape(B, STEPS, S)

    def advance(probs):
        def one_block(total, index):
            start = (index * block_rows).astype(jnp.int32)
            rows = lax.dynamic_slice_in_dim(src_emb, start, block_rows, 0)
            logits = jnp.dot(rows, dst_emb.T, preferred_element_type=jnp.float32)
            top = jnp.max(logits, axis=1)
            shifted = jnp.exp(logits - top[:, None])
            row_total = jnp.sum(shifted, axis=1)
            trans = shifted.astype(jnp.bfloat16)
            part = lax.dynamic_slice_in_dim(probs, start, block_rows, 1).astype(jnp.float32)
            weights = (part / row_total[None, :]).astype(jnp.bfloat16)
            return total + jnp.dot(weights, trans, preferred_element_type=jnp.float32), None

        result, _ = lax.scan(one_block, jnp.zeros((B, S), jnp.float32), jnp.arange(block_count, dtype=jnp.int32))
        return result

    joint1 = advance(start_probs) * emit[:, 0]
    scale1 = jnp.sum(joint1, axis=1) / S
    probs1 = (joint1 / scale1[:, None]).astype(jnp.bfloat16)
    joint2 = advance(probs1) * emit[:, 1]
    scale2 = jnp.sum(joint2, axis=1) / S
    final_probs = joint2 / scale2[:, None]
    log_norm = jnp.log(scale1) + jnp.log(scale2)
    return final_probs, log_norm
```

```python
import functools

import jax
import jax.numpy as jnp
from jax import lax
from jax.experimental import pallas as pl
from jax.experimental.pallas import tpu as pltpu
from jax.sharding import PartitionSpec as P

F32 = jnp.float32
BF16 = jnp.bfloat16
NT = (((1,), (1,)), ((), ()))
SPREAD = 60.0
VMEM_LIMIT = 48 * 1024 * 1024


def block_of(count, most):
    return max(size for size in range(16, most + 1, 16) if count % size == 0)


def params():
    return pltpu.CompilerParams(
        vmem_limit_bytes=VMEM_LIMIT, dimension_semantics=("arbitrary",)
    )


def logits_of(rows, columns):
    return lax.dot_general(rows, columns, NT, preferred_element_type=F32)


def stats_kernel(x_ref, y_ref, top_ref, total_ref, buf0, buf1, *, rows, sub):
    count, columns = x_ref.shape[0], y_ref.shape[0]
    bufs = (buf0, buf1)
    head = min(rows, 256)
    units = [(c, a) for c in range(0, columns, sub) for a in range(0, count, rows)]

    def multiply(unit, buf):
        c, a = unit
        logits = logits_of(x_ref[a : a + rows, :], y_ref[c : c + sub, :])
        buf[...] = logits
        top = jnp.max(logits.reshape(rows // 8, 8, sub), axis=0)
        shift = jnp.max(logits[:head], axis=0, keepdims=True) if a == 0 else None
        return top, shift

    worst = jnp.zeros((1, sub), F32)
    upcoming = multiply(units[0], buf0)
    top = total = shift = None
    for k, (c, a) in enumerate(units):
        unit_top, unit_shift = upcoming
        if a == 0:
            shift, top = unit_shift, unit_top
        else:
            top = jnp.maximum(top, unit_top)
        if k + 1 < len(units):
            upcoming = multiply(units[k + 1], bufs[(k + 1) % 2])
        part = jnp.sum(jnp.exp(bufs[k % 2][...] - shift).reshape(rows // 8, 8, sub), axis=0)
        total = part if a == 0 else total + part
        if a + rows == count:
            total = jnp.sum(total, axis=0, keepdims=True)
            top = jnp.max(top, axis=0, keepdims=True)
            worst = jnp.maximum(worst, top - shift)
            top_ref[:, c : c + sub] = top
            total_ref[:, c : c + sub] = total / jnp.exp(top - shift)

    @pl.when(jnp.max(worst) > SPREAD)
    def again():
        for c in range(0, columns, sub):

            def logits_at(k):
                part = x_ref[pl.ds(pl.multiple_of(k * rows, rows), rows), :]
                return logits_of(part, y_ref[c : c + sub, :])

            def max_step(k, so_far):
                return jnp.maximum(so_far, jnp.max(logits_at(k), axis=0, keepdims=True))

            top = lax.fori_loop(0, count // rows, max_step, jnp.full((1, sub), -jnp.inf, F32))

            def sum_step(k, so_far):
                return so_far + jnp.sum(jnp.exp(logits_at(k) - top), axis=0, keepdims=True)

            total = lax.fori_loop(0, count // rows, sum_step, jnp.zeros((1, sub), F32))
            top_ref[:, c : c + sub] = top
            total_ref[:, c : c + sub] = total


def column_stats(x, y, name):
    count, depth = x.shape
    columns = y.shape[0]
    width = block_of(columns, 1024)
    sub = block_of(width, 256)
    rows = block_of(count, 1024)
    return pl.pallas_call(
        functools.partial(stats_kernel, rows=rows, sub=sub),
        grid=(columns // width,),
        in_specs=[
            pl.BlockSpec((count, depth), lambda i: (0, 0)),
            pl.BlockSpec((width, depth), lambda i: (i, 0)),
        ],
        out_specs=[pl.BlockSpec((1, width), lambda i: (0, i))] * 2,
        out_shape=[jax.ShapeDtypeStruct((1, columns), F32)] * 2,
        scratch_shapes=[pltpu.VMEM((rows, sub), F32)] * 2,
        compiler_params=params(),
        cost_estimate=pl.CostEstimate(
            flops=2 * count * columns * depth,
            bytes_accessed=2 * depth * (count + columns),
            transcendentals=count * columns,
        ),
        name=name,
    )(x, y)


def trans_kernel(src_ref, dst_ref, top_ref, weight_ref, trans_ref, out_ref, buf0, buf1, *, cols):
    count = dst_ref.shape[0] // cols
    bufs = (buf0, buf1)

    @pl.when(pl.program_id(0) == 0)
    def _():
        out_ref[...] = jnp.zeros_like(out_ref)

    def multiply(k):
        bufs[k % 2][...] = logits_of(src_ref[...], dst_ref[k * cols : (k + 1) * cols, :])

    def advance(k):
        here = slice(k * cols, (k + 1) * cols)
        out_ref[:, here] += jnp.dot(
            weight_ref[...], trans_ref[:, here], preferred_element_type=F32
        )

    multiply(0)
    for k in range(count):
        if k + 1 < count:
            multiply(k + 1)
        shifted = jnp.exp(bufs[k % 2][...] - top_ref[...])
        trans_ref[:, k * cols : (k + 1) * cols] = shifted.astype(BF16)
        if k > 0:
            advance(k - 1)
    advance(count - 1)


def build_and_advance(src, dst, top, weights):
    sources, depth = src.shape
    dests = dst.shape[0]
    batch = weights.shape[0]
    rows = block_of(sources, 1024)
    cols = block_of(dests, 256)
    return pl.pallas_call(
        functools.partial(trans_kernel, cols=cols),
        grid=(sources // rows,),
        in_specs=[
            pl.BlockSpec((rows, depth), lambda i: (i, 0)),
            pl.BlockSpec((dests, depth), lambda i: (0, 0)),
            pl.BlockSpec((rows, 1), lambda i: (i, 0)),
            pl.BlockSpec((batch, rows), lambda i: (0, i)),
        ],
        out_specs=[
            pl.BlockSpec((rows, dests), lambda i: (i, 0)),
            pl.BlockSpec((batch, dests), lambda i: (0, 0)),
        ],
        out_shape=[
            jax.ShapeDtypeStruct((sources, dests), BF16),
            jax.ShapeDtypeStruct((batch, dests), F32),
        ],
        scratch_shapes=[pltpu.VMEM((rows, cols), F32)] * 2,
        compiler_params=params(),
        cost_estimate=pl.CostEstimate(
            flops=2 * sources * dests * (depth + batch),
            bytes_accessed=2 * sources * dests,
            transcendentals=sources * dests,
        ),
        name="build_trans",
    )(src, dst, top, weights)


def advance_kernel(weight_ref, trans_ref, out_ref):
    @pl.when(pl.program_id(0) == 0)
    def _():
        out_ref[...] = jnp.zeros_like(out_ref)

    out_ref[...] += jnp.dot(weight_ref[...], trans_ref[...], preferred_element_type=F32)


def advance(weights, trans):
    sources, dests = trans.shape
    batch = weights.shape[0]
    rows = block_of(sources, 2048)
    return pl.pallas_call(
        advance_kernel,
        grid=(sources // rows,),
        in_specs=[
            pl.BlockSpec((batch, rows), lambda i: (0, i)),
            pl.BlockSpec((rows, dests), lambda i: (i, 0)),
        ],
        out_specs=pl.BlockSpec((batch, dests), lambda i: (0, 0)),
        out_shape=jax.ShapeDtypeStruct((batch, dests), F32),
        compiler_params=params(),
        cost_estimate=pl.CostEstimate(
            flops=2 * sources * dests * batch,
            bytes_accessed=2 * sources * dests,
            transcendentals=0,
        ),
        name="advance",
    )(weights, trans)


def bits_of(count):
    return [1 << k for k in range(count.bit_length() - 1)]


def swapped(value, axis, mask):
    count = lax.axis_size(axis)
    return lax.ppermute(value, axis, [(i, i ^ mask) for i in range(count)])


def summed_all(value, axes):
    for axis in axes:
        for mask in bits_of(lax.axis_size(axis)):
            value = value + swapped(value, axis, mask)
    return value


def merged_rows(stats, rows):
    others = [swapped(stats, "row", mask) for mask in range(1, rows)]
    top = functools.reduce(jnp.maximum, [part[0] for part in others], stats[0])
    totals = [part[1] * jnp.exp(part[0] - top) for part in [stats] + others]
    while len(totals) > 1:
        totals = [first + second for first, second in zip(totals[::2], totals[1::2])]
    return top, totals[0]


def tied(value, others):
    return lax.optimization_barrier((value, *others))[0]


def widths_of(dests):
    unit = block_of(dests, 256)
    count = dests // unit
    last = max(1, count // 8)
    rest = count - last
    first = [rest // 3 + (k < rest % 3) for k in range(3)]
    return [unit * size for size in first + [last] if size]


def add(value, received):
    return value + received


def root_hops(rows, cols):
    per_row = cols // rows
    hops = []
    for hop in range(1, rows):
        perm = []
        for col in range(cols):
            root = col // per_row
            if hop <= root:
                perm.append(((hop - 1) * cols + col, hop * cols + col))
            if hop <= rows - 1 - root:
                perm.append(((rows - hop) * cols + col, (rows - hop - 1) * cols + col))
        hops.append((lambda value, perm=perm: lax.ppermute(value, ("row", "col"), perm), add))
    return hops


def everywhere_hops(middle):
    return [
        (lambda value: lax.ppermute(value, "row", [(0, 1), (3, 2)]), add),
        (lambda value: lax.ppermute(value, "row", [(1, 2), (2, 1)]), add),
        (
            lambda value: lax.ppermute(value, "row", [(1, 0), (2, 3)]),
            lambda value, received: jnp.where(middle, value, received),
        ),
    ]


def piped(compute, operand, count, hops, small, rounds):
    moving, ready = [], []
    for k in range(count):
        part = compute(k, tied(operand, ready) if ready else operand)
        received = [hops[at][0](value) if at < len(hops) else value for value, at in moving]
        part, *received = lax.optimization_barrier((part, *received))
        moving = [
            (hops[at][1](value, got), at + 1) if at < len(hops) else (value, at)
            for (value, at), got in zip(moving, received)
        ]
        ready = [value for value, at in moving]
        moving.append((part, 0))
    small = small()
    for k in range(len(hops)):
        received = [hops[at][0](value) if at < len(hops) else value for value, at in moving]
        for step in rounds[k]:
            small = step(small)
        small, *received = lax.optimization_barrier((small, *received))
        moving = [
            (hops[at][1](value, got), at + 1) if at < len(hops) else (value, at)
            for (value, at), got in zip(moving, received)
        ]
    return [value for value, at in moving], small


def to_sources(block, rows, cols):
    per_row = cols // rows
    row, col = lax.axis_index("row"), lax.axis_index("col")
    group = col // per_row
    relation = group ^ row
    half = block.shape[1] // 2
    first, second = block[:, :half], block[:, half:]

    def sent(value, pairs):
        at = lambda r, mask, m: r * cols + (r ^ mask) * per_row + m
        perm = [
            (at(r, a, m), at(r, b, m)) for r in range(rows) for a, b in pairs for m in range(per_row)
        ]
        return lax.ppermute(value, ("row", "col"), perm)

    first = jnp.where(relation == 0, first, sent(first, [(0, 1)]))
    second = jnp.where(relation == 0, second, sent(second, [(0, 2)]))
    first = jnp.where(relation <= 1, first, sent(first, [(0, 2), (1, 3)]))
    second = jnp.where((relation == 0) | (relation == 2), second, sent(second, [(0, 1), (2, 3)]))
    blocks = jnp.concatenate([first, second], axis=1)
    member = col % per_row
    for mask in bits_of(per_row):
        other = swapped(blocks, "col", mask)
        blocks = jnp.where(
            member & mask == 0,
            jnp.concatenate([blocks, other], axis=1),
            jnp.concatenate([other, blocks], axis=1),
        )
    return blocks


def on_device(src_emb, dst_emb, state_emb, word_emb, start_probs, token_ids):
    rows, cols = lax.axis_size("row"), lax.axis_size("col")
    row = lax.axis_index("row")
    middle = (row == 1) | (row == 2)
    batch, steps = token_ids.shape
    dests = dst_emb.shape[0]
    states = dests * cols

    src_rows = lax.all_gather(src_emb, "col", axis=0, tiled=True)

    vocab = jnp.stack(column_stats(word_emb, state_emb, "vocab_stats"))
    vocab_top, vocab_total = merged_rows(vocab, rows)
    state_norm = vocab_top + jnp.log(vocab_total)

    vocab_rows = word_emb.shape[0]
    flat_ids = token_ids.T.reshape(-1) - row * vocab_rows
    onehot = (flat_ids[:, None] == jnp.arange(vocab_rows, dtype=jnp.int32)[None, :]).astype(BF16)
    picked = jnp.dot(onehot, word_emb, preferred_element_type=F32).astype(BF16)
    token_vecs = summed_all(picked, ("row",))
    scores = logits_of(token_vecs, state_emb)
    emit = jnp.exp(scores - state_norm)

    stats = jnp.stack(column_stats(dst_emb, src_rows, "trans_stats"))
    every = lax.all_gather(stats, "col")
    row_top = jnp.max(every[:, 0], axis=0)
    row_total = jnp.sum(every[:, 1] * jnp.exp(every[:, 0] - row_top[None]), axis=0)

    weights0 = (start_probs.astype(F32) / row_total).astype(BF16)
    top_column = row_top.reshape(-1, 1)
    widths = widths_of(dests)
    starts = [sum(widths[:k]) for k in range(len(widths))]
    here = [slice(at, at + width) for at, width in zip(starts, widths)]

    trans, scales1 = [], []

    def add_over(axis, mask):
        return lambda value: value + swapped(value, axis, mask)

    def add_rows(value):
        if rows != 4:
            return summed_all(value, ("row",))
        one, two, three = [swapped(value, "row", mask) for mask in (1, 2, 3)]
        return (value + one) + (two + three)

    col_rounds = [add_over("col", mask) for mask in bits_of(cols)]

    def first_step(k, weights):
        built, part = build_and_advance(src_rows, dst_emb[here[k]], top_column, weights)
        trans.append(built)
        scales1.append(jnp.sum(part * emit[:batch, here[k]], axis=1))
        return part

    sums1, scale1 = piped(
        first_step,
        weights0,
        len(widths),
        root_hops(rows, cols),
        lambda: sum(scales1),
        [col_rounds, [add_rows], []],
    )
    scale1 = scale1 / states
    joint1 = jnp.concatenate(sums1, axis=1) * emit[:batch]
    probs1 = (joint1 / scale1[:, None]).astype(BF16)
    source_probs = to_sources(probs1, rows, cols)
    weights1 = (source_probs.astype(F32) / row_total).astype(BF16)

    def second_step(k, weights):
        return advance(weights, trans[k])

    sums2, _ = piped(
        second_step,
        weights1,
        len(widths),
        everywhere_hops(middle),
        lambda: scale1,
        [[], [], []],
    )
    joint2 = jnp.concatenate(sums2, axis=1) * emit[batch : 2 * batch]
    scale2 = summed_all(jnp.sum(joint2, axis=1), ("col",)) / states
    final_probs = joint2 / scale2[:, None]
    log_norm = jnp.log(scale1) + jnp.log(scale2)
    return (final_probs, log_norm)


def solution(mesh):
    in_specs = (
        P(("row", "col"), None),
        P("col", None),
        P("col", None),
        P("row", None),
        P(None, "row"),
        P(),
    )
    out_specs = (P(None, "col"), P())
    return jax.shard_map(
        on_device, mesh=mesh, in_specs=in_specs, out_specs=out_specs, check_vma=False
    )
```

```python
import functools

import jax
import jax.numpy as jnp
from jax import lax
from jax.experimental import pallas as pl
from jax.experimental.pallas import tpu as pltpu
from jax.sharding import PartitionSpec as P

F32 = jnp.float32
BF16 = jnp.bfloat16
NT = (((1,), (1,)), ((), ()))
SPREAD = 60.0
VMEM_LIMIT = 48 * 1024 * 1024


def block_of(count, most):
    return max(size for size in range(16, most + 1, 16) if count % size == 0)


def params():
    return pltpu.CompilerParams(
        vmem_limit_bytes=VMEM_LIMIT, dimension_semantics=("arbitrary",)
    )


def logits_of(rows, columns):
    return lax.dot_general(rows, columns, NT, preferred_element_type=F32)


def stats_kernel(x_ref, y_ref, top_ref, total_ref, buf0, buf1, *, rows, sub):
    count, columns = x_ref.shape[0], y_ref.shape[0]
    bufs = (buf0, buf1)
    head = min(rows, 256)
    units = [(c, a) for c in range(0, columns, sub) for a in range(0, count, rows)]

    def multiply(unit, buf):
        c, a = unit
        logits = logits_of(x_ref[a : a + rows, :], y_ref[c : c + sub, :])
        buf[...] = logits
        top = jnp.max(logits.reshape(rows // 8, 8, sub), axis=0)
        shift = jnp.max(logits[:head], axis=0, keepdims=True) if a == 0 else None
        return top, shift

    worst = jnp.zeros((1, sub), F32)
    upcoming = multiply(units[0], buf0)
    top = total = shift = None
    for k, (c, a) in enumerate(units):
        unit_top, unit_shift = upcoming
        if a == 0:
            shift, top = unit_shift, unit_top
        else:
            top = jnp.maximum(top, unit_top)
        if k + 1 < len(units):
            upcoming = multiply(units[k + 1], bufs[(k + 1) % 2])
        part = jnp.sum(jnp.exp(bufs[k % 2][...] - shift).reshape(rows // 8, 8, sub), axis=0)
        total = part if a == 0 else total + part
        if a + rows == count:
            total = jnp.sum(total, axis=0, keepdims=True)
            top = jnp.max(top, axis=0, keepdims=True)
            worst = jnp.maximum(worst, top - shift)
            top_ref[:, c : c + sub] = top
            total_ref[:, c : c + sub] = total / jnp.exp(top - shift)

    @pl.when(jnp.max(worst) > SPREAD)
    def again():
        for c in range(0, columns, sub):

            def logits_at(k):
                part = x_ref[pl.ds(pl.multiple_of(k * rows, rows), rows), :]
                return logits_of(part, y_ref[c : c + sub, :])

            def max_step(k, so_far):
                return jnp.maximum(so_far, jnp.max(logits_at(k), axis=0, keepdims=True))

            top = lax.fori_loop(0, count // rows, max_step, jnp.full((1, sub), -jnp.inf, F32))

            def sum_step(k, so_far):
                return so_far + jnp.sum(jnp.exp(logits_at(k) - top), axis=0, keepdims=True)

            total = lax.fori_loop(0, count // rows, sum_step, jnp.zeros((1, sub), F32))
            top_ref[:, c : c + sub] = top
            total_ref[:, c : c + sub] = total


def column_stats(x, y, name):
    count, depth = x.shape
    columns = y.shape[0]
    width = block_of(columns, 1024)
    sub = block_of(width, 256)
    rows = block_of(count, 1024)
    return pl.pallas_call(
        functools.partial(stats_kernel, rows=rows, sub=sub),
        grid=(columns // width,),
        in_specs=[
            pl.BlockSpec((count, depth), lambda i: (0, 0)),
            pl.BlockSpec((width, depth), lambda i: (i, 0)),
        ],
        out_specs=[pl.BlockSpec((1, width), lambda i: (0, i))] * 2,
        out_shape=[jax.ShapeDtypeStruct((1, columns), F32)] * 2,
        scratch_shapes=[pltpu.VMEM((rows, sub), F32)] * 2,
        compiler_params=params(),
        cost_estimate=pl.CostEstimate(
            flops=2 * count * columns * depth,
            bytes_accessed=2 * depth * (count + columns),
            transcendentals=count * columns,
        ),
        name=name,
    )(x, y)


def trans_kernel(src_ref, dst_ref, top_ref, weight_ref, trans_ref, out_ref, buf0, buf1, *, cols):
    count = dst_ref.shape[0] // cols
    bufs = (buf0, buf1)

    @pl.when(pl.program_id(0) == 0)
    def _():
        out_ref[...] = jnp.zeros_like(out_ref)

    def multiply(k):
        bufs[k % 2][...] = logits_of(src_ref[...], dst_ref[k * cols : (k + 1) * cols, :])

    def advance(k):
        here = slice(k * cols, (k + 1) * cols)
        out_ref[:, here] += jnp.dot(
            weight_ref[...], trans_ref[:, here], preferred_element_type=F32
        )

    multiply(0)
    for k in range(count):
        if k + 1 < count:
            multiply(k + 1)
        shifted = jnp.exp(bufs[k % 2][...] - top_ref[...])
        trans_ref[:, k * cols : (k + 1) * cols] = shifted.astype(BF16)
        if k > 0:
            advance(k - 1)
    advance(count - 1)


def build_and_advance(src, dst, top, weights):
    sources, depth = src.shape
    dests = dst.shape[0]
    batch = weights.shape[0]
    rows = block_of(sources, 1024)
    cols = block_of(dests, 256)
    return pl.pallas_call(
        functools.partial(trans_kernel, cols=cols),
        grid=(sources // rows,),
        in_specs=[
            pl.BlockSpec((rows, depth), lambda i: (i, 0)),
            pl.BlockSpec((dests, depth), lambda i: (0, 0)),
            pl.BlockSpec((rows, 1), lambda i: (i, 0)),
            pl.BlockSpec((batch, rows), lambda i: (0, i)),
        ],
        out_specs=[
            pl.BlockSpec((rows, dests), lambda i: (i, 0)),
            pl.BlockSpec((batch, dests), lambda i: (0, 0)),
        ],
        out_shape=[
            jax.ShapeDtypeStruct((sources, dests), BF16),
            jax.ShapeDtypeStruct((batch, dests), F32),
        ],
        scratch_shapes=[pltpu.VMEM((rows, cols), F32)] * 2,
        compiler_params=params(),
        cost_estimate=pl.CostEstimate(
            flops=2 * sources * dests * (depth + batch),
            bytes_accessed=2 * sources * dests,
            transcendentals=sources * dests,
        ),
        name="build_trans",
    )(src, dst, top, weights)


def advance_kernel(weight_ref, *refs):
    trans_refs, out_ref = refs[:-1], refs[-1]

    @pl.when(pl.program_id(0) == 0)
    def _():
        out_ref[...] = jnp.zeros_like(out_ref)

    at = 0
    for trans_ref in trans_refs:
        here = slice(at, at + trans_ref.shape[1])
        out_ref[:, here] += jnp.dot(weight_ref[...], trans_ref[...], preferred_element_type=F32)
        at += trans_ref.shape[1]


def advance(weights, trans):
    sources = trans[0].shape[0]
    dests = sum(part.shape[1] for part in trans)
    batch = weights.shape[0]
    rows = block_of(sources, 1024)
    return pl.pallas_call(
        advance_kernel,
        grid=(sources // rows,),
        in_specs=[pl.BlockSpec((batch, rows), lambda i: (0, i))]
        + [pl.BlockSpec((rows, part.shape[1]), lambda i: (i, 0)) for part in trans],
        out_specs=pl.BlockSpec((batch, dests), lambda i: (0, 0)),
        out_shape=jax.ShapeDtypeStruct((batch, dests), F32),
        compiler_params=params(),
        cost_estimate=pl.CostEstimate(
            flops=2 * sources * dests * batch,
            bytes_accessed=2 * sources * dests,
            transcendentals=0,
        ),
        name="advance",
    )(weights, *trans)


def bits_of(count):
    return [1 << k for k in range(count.bit_length() - 1)]


def swapped(value, axis, mask):
    count = lax.axis_size(axis)
    return lax.ppermute(value, axis, [(i, i ^ mask) for i in range(count)])


def summed_all(value, axes):
    for axis in axes:
        for mask in bits_of(lax.axis_size(axis)):
            value = value + swapped(value, axis, mask)
    return value


def merged_rows(stats, rows):
    others = [swapped(stats, "row", mask) for mask in range(1, rows)]
    top = functools.reduce(jnp.maximum, [part[0] for part in others], stats[0])
    totals = [part[1] * jnp.exp(part[0] - top) for part in [stats] + others]
    while len(totals) > 1:
        totals = [first + second for first, second in zip(totals[::2], totals[1::2])]
    return top, totals[0]


def tied(value, others):
    return lax.optimization_barrier((value, *others))[0]


def widths_of(dests):
    unit = block_of(dests, 256)
    count = dests // unit
    first = max(1, count * 5 // 8)
    return [unit * size for size in (first, count - first) if size]


def root_hops(rows, cols):
    per_row = cols // rows
    if rows == 4:
        lines = {
            0: ([(1, 0), (3, 2)], [(2, 0)]),
            1: ([(0, 1), (3, 2)], [(2, 1)]),
            2: ([(0, 1), (3, 2)], [(1, 2)]),
            3: ([(0, 1), (2, 3)], [(1, 3)]),
        }
    else:
        lines = {
            root: [[(at, root)] for at in range(rows) if at != root] for root in range(rows)
        }
    hops = []
    for hop in range(len(lines[0])):
        perm = [
            (a * cols + col, b * cols + col)
            for col in range(cols)
            for a, b in lines[col // per_row][hop]
        ]
        hops.append(lambda value, perm=perm: lax.ppermute(value, ("row", "col"), perm))
    return hops


def piped(compute, operand, count, hops, small, rounds):
    moving, ready = [], []

    def moved(beside):
        received = [hops[at](value) for value, at in moving if at < len(hops)]
        beside, *received = lax.optimization_barrier((beside(), *received))
        received.reverse()
        return beside, [
            (value + received.pop(), at + 1) if at < len(hops) else (value, at)
            for value, at in moving
        ]

    for k in range(count):
        part, moving = moved(lambda: compute(k, tied(operand, ready) if ready else operand))
        ready = [value for value, at in moving]
        moving.append((part, 0))
    small = small()
    for k in range(len(hops)):

        def beside():
            value = small
            for step in rounds[k]:
                value = step(value)
            return value

        small, moving = moved(beside)
    return [value for value, at in moving], small


def to_sources(block, rows, cols):
    per_row = cols // rows
    row, col = lax.axis_index("row"), lax.axis_index("col")
    group = col // per_row
    relation = group ^ row
    half = block.shape[1] // 2
    first, second = block[:, :half], block[:, half:]

    def sent(value, pairs):
        at = lambda r, mask, m: r * cols + (r ^ mask) * per_row + m
        perm = [
            (at(r, a, m), at(r, b, m)) for r in range(rows) for a, b in pairs for m in range(per_row)
        ]
        return lax.ppermute(value, ("row", "col"), perm)

    near, far = lax.optimization_barrier((sent(first, [(0, 1)]), sent(second, [(0, 2)])))
    first = jnp.where(relation == 0, first, near)
    second = jnp.where(relation == 0, second, far)
    far, near = lax.optimization_barrier(
        (sent(first, [(0, 2), (1, 3)]), sent(second, [(0, 1), (2, 3)]))
    )
    first = jnp.where(relation <= 1, first, far)
    second = jnp.where((relation == 0) | (relation == 2), second, near)
    blocks = jnp.concatenate([first, second], axis=1)
    member = col % per_row
    for mask in bits_of(per_row):
        other = swapped(blocks, "col", mask)
        blocks = jnp.where(
            member & mask == 0,
            jnp.concatenate([blocks, other], axis=1),
            jnp.concatenate([other, blocks], axis=1),
        )
    return blocks


def on_device(src_emb, dst_emb, state_emb, word_emb, start_probs, token_ids):
    rows, cols = lax.axis_size("row"), lax.axis_size("col")
    row = lax.axis_index("row")
    batch, steps = token_ids.shape
    dests = dst_emb.shape[0]
    states = dests * cols

    src_rows = lax.all_gather(src_emb, "col", axis=0, tiled=True)

    vocab = jnp.stack(column_stats(word_emb, state_emb, "vocab_stats"))
    vocab_top, vocab_total = merged_rows(vocab, rows)
    state_norm = vocab_top + jnp.log(vocab_total)

    vocab_rows = word_emb.shape[0]
    flat_ids = token_ids.T.reshape(-1) - row * vocab_rows
    onehot = (flat_ids[:, None] == jnp.arange(vocab_rows, dtype=jnp.int32)[None, :]).astype(BF16)
    picked = jnp.dot(onehot, word_emb, preferred_element_type=F32).astype(BF16)
    token_vecs = summed_all(picked, ("row",))
    scores = logits_of(token_vecs, state_emb)
    emit = jnp.exp(scores - state_norm)

    stats = jnp.stack(column_stats(dst_emb, src_rows, "trans_stats"))
    every = lax.all_gather(stats, "col")
    row_top = jnp.max(every[:, 0], axis=0)
    row_total = jnp.sum(every[:, 1] * jnp.exp(every[:, 0] - row_top[None]), axis=0)

    weights0 = (start_probs.astype(F32) / row_total).astype(BF16)
    top_column = row_top.reshape(-1, 1)
    widths = widths_of(dests)
    starts = [sum(widths[:k]) for k in range(len(widths))]
    here = [slice(at, at + width) for at, width in zip(starts, widths)]

    trans, scales1 = [], []

    def add_rows(value):
        if rows != 4:
            return summed_all(value, ("row",))
        one, two, three = [swapped(value, "row", mask) for mask in (1, 2, 3)]
        return (value + one) + (two + three)


    def add_over(axis, mask):
        return lambda value: value + swapped(value, axis, mask)

    col_rounds = [add_over("col", mask) for mask in bits_of(cols)]

    def first_step(k, weights):
        built, part = build_and_advance(src_rows, dst_emb[here[k]], top_column, weights)
        trans.append(built)
        scales1.append(jnp.sum(part * emit[:batch, here[k]], axis=1))
        return part

    rounds = [col_rounds, [add_rows]] + [[]] * rows
    sums1, scale1 = piped(
        first_step,
        weights0,
        len(widths),
        root_hops(rows, cols),
        lambda: sum(scales1),
        rounds,
    )
    scale1 = scale1 / states
    joint1 = jnp.concatenate(sums1, axis=1) * emit[:batch]
    probs1 = (joint1 / scale1[:, None]).astype(BF16)
    source_probs = to_sources(probs1, rows, cols)
    weights1 = (source_probs.astype(F32) / row_total).astype(BF16)

    part = advance(weights1, trans)
    sums2 = lax.psum(part, "row")
    scale2 = summed_all(jnp.sum(part * emit[batch : 2 * batch], axis=1), ("col", "row"))
    scale2 = scale2 / states
    final_probs = sums2 * emit[batch : 2 * batch] / scale2[:, None]
    log_norm = jnp.log(scale1) + jnp.log(scale2)
    return (final_probs, log_norm)


def solution(mesh):
    in_specs = (
        P(("row", "col"), None),
        P("col", None),
        P("col", None),
        P("row", None),
        P(None, "row"),
        P(),
    )
    out_specs = (P(None, "col"), P())
    return jax.shard_map(
        on_device, mesh=mesh, in_specs=in_specs, out_specs=out_specs, check_vma=False
    )
```

```python
import functools

import jax
import jax.numpy as jnp
from jax import lax
from jax.experimental import pallas as pl
from jax.experimental.pallas import tpu as pltpu
from jax.sharding import PartitionSpec as P

F32 = jnp.float32
BF16 = jnp.bfloat16
NT = (((1,), (1,)), ((), ()))
SPREAD = 60.0
VMEM_LIMIT = 48 * 1024 * 1024


def block_of(count, most):
    return max(size for size in range(16, most + 1, 16) if count % size == 0)


def params():
    return pltpu.CompilerParams(
        vmem_limit_bytes=VMEM_LIMIT, dimension_semantics=("arbitrary",)
    )


def logits_of(rows, columns):
    return lax.dot_general(rows, columns, NT, preferred_element_type=F32)


def stats_kernel(x_ref, y_ref, top_ref, total_ref, buf0, buf1, *, rows, sub):
    count, columns = x_ref.shape[0], y_ref.shape[0]
    bufs = (buf0, buf1)
    head = min(rows, 256)
    units = [(c, a) for c in range(0, columns, sub) for a in range(0, count, rows)]

    def multiply(unit, buf):
        c, a = unit
        logits = logits_of(x_ref[a : a + rows, :], y_ref[c : c + sub, :])
        buf[...] = logits
        top = jnp.max(logits.reshape(rows // 8, 8, sub), axis=0)
        shift = jnp.max(logits[:head], axis=0, keepdims=True) if a == 0 else None
        return top, shift

    worst = jnp.zeros((1, sub), F32)
    upcoming = multiply(units[0], buf0)
    top = total = shift = None
    for k, (c, a) in enumerate(units):
        unit_top, unit_shift = upcoming
        if a == 0:
            shift, top = unit_shift, unit_top
        else:
            top = jnp.maximum(top, unit_top)
        if k + 1 < len(units):
            upcoming = multiply(units[k + 1], bufs[(k + 1) % 2])
        part = jnp.sum(jnp.exp(bufs[k % 2][...] - shift).reshape(rows // 8, 8, sub), axis=0)
        total = part if a == 0 else total + part
        if a + rows == count:
            total = jnp.sum(total, axis=0, keepdims=True)
            top = jnp.max(top, axis=0, keepdims=True)
            worst = jnp.maximum(worst, top - shift)
            top_ref[:, c : c + sub] = top
            total_ref[:, c : c + sub] = total / jnp.exp(top - shift)

    @pl.when(jnp.max(worst) > SPREAD)
    def again():
        for c in range(0, columns, sub):

            def logits_at(k):
                part = x_ref[pl.ds(pl.multiple_of(k * rows, rows), rows), :]
                return logits_of(part, y_ref[c : c + sub, :])

            def max_step(k, so_far):
                return jnp.maximum(so_far, jnp.max(logits_at(k), axis=0, keepdims=True))

            top = lax.fori_loop(0, count // rows, max_step, jnp.full((1, sub), -jnp.inf, F32))

            def sum_step(k, so_far):
                return so_far + jnp.sum(jnp.exp(logits_at(k) - top), axis=0, keepdims=True)

            total = lax.fori_loop(0, count // rows, sum_step, jnp.zeros((1, sub), F32))
            top_ref[:, c : c + sub] = top
            total_ref[:, c : c + sub] = total


def column_stats(x, y, name):
    count, depth = x.shape
    columns = y.shape[0]
    width = block_of(columns, 1024)
    sub = block_of(width, 256)
    rows = block_of(count, 1024)
    return pl.pallas_call(
        functools.partial(stats_kernel, rows=rows, sub=sub),
        grid=(columns // width,),
        in_specs=[
            pl.BlockSpec((count, depth), lambda i: (0, 0)),
            pl.BlockSpec((width, depth), lambda i: (i, 0)),
        ],
        out_specs=[pl.BlockSpec((1, width), lambda i: (0, i))] * 2,
        out_shape=[jax.ShapeDtypeStruct((1, columns), F32)] * 2,
        scratch_shapes=[pltpu.VMEM((rows, sub), F32)] * 2,
        compiler_params=params(),
        cost_estimate=pl.CostEstimate(
            flops=2 * count * columns * depth,
            bytes_accessed=2 * depth * (count + columns),
            transcendentals=count * columns,
        ),
        name=name,
    )(x, y)


def trans_kernel(src_ref, dst_ref, top_ref, weight_ref, trans_ref, out_ref, buf0, buf1, *, cols):
    count = dst_ref.shape[0] // cols
    bufs = (buf0, buf1)

    @pl.when(pl.program_id(0) == 0)
    def _():
        out_ref[...] = jnp.zeros_like(out_ref)

    def multiply(k):
        bufs[k % 2][...] = logits_of(src_ref[...], dst_ref[k * cols : (k + 1) * cols, :])

    def advance(k):
        here = slice(k * cols, (k + 1) * cols)
        out_ref[:, here] += jnp.dot(
            weight_ref[...], trans_ref[:, here], preferred_element_type=F32
        )

    multiply(0)
    for k in range(count):
        if k + 1 < count:
            multiply(k + 1)
        shifted = jnp.exp(bufs[k % 2][...] - top_ref[...])
        trans_ref[:, k * cols : (k + 1) * cols] = shifted.astype(BF16)
        if k > 0:
            advance(k - 1)
    advance(count - 1)


def build_and_advance(src, dst, top, weights):
    sources, depth = src.shape
    dests = dst.shape[0]
    batch = weights.shape[0]
    rows = block_of(sources, 1024)
    cols = block_of(dests, 256)
    return pl.pallas_call(
        functools.partial(trans_kernel, cols=cols),
        grid=(sources // rows,),
        in_specs=[
            pl.BlockSpec((rows, depth), lambda i: (i, 0)),
            pl.BlockSpec((dests, depth), lambda i: (0, 0)),
            pl.BlockSpec((rows, 1), lambda i: (i, 0)),
            pl.BlockSpec((batch, rows), lambda i: (0, i)),
        ],
        out_specs=[
            pl.BlockSpec((rows, dests), lambda i: (i, 0)),
            pl.BlockSpec((batch, dests), lambda i: (0, 0)),
        ],
        out_shape=[
            jax.ShapeDtypeStruct((sources, dests), BF16),
            jax.ShapeDtypeStruct((batch, dests), F32),
        ],
        scratch_shapes=[pltpu.VMEM((rows, cols), F32)] * 2,
        compiler_params=params(),
        cost_estimate=pl.CostEstimate(
            flops=2 * sources * dests * (depth + batch),
            bytes_accessed=2 * sources * dests,
            transcendentals=sources * dests,
        ),
        name="build_trans",
    )(src, dst, top, weights)


def advance_kernel(weight_ref, trans_ref, out_ref):
    @pl.when(pl.program_id(0) == 0)
    def _():
        out_ref[...] = jnp.zeros_like(out_ref)

    out_ref[...] += jnp.dot(weight_ref[...], trans_ref[...], preferred_element_type=F32)


def advance(weights, trans):
    sources, dests = trans.shape
    batch = weights.shape[0]
    rows = block_of(sources, 2048)
    return pl.pallas_call(
        advance_kernel,
        grid=(sources // rows,),
        in_specs=[
            pl.BlockSpec((batch, rows), lambda i: (0, i)),
            pl.BlockSpec((rows, dests), lambda i: (i, 0)),
        ],
        out_specs=pl.BlockSpec((batch, dests), lambda i: (0, 0)),
        out_shape=jax.ShapeDtypeStruct((batch, dests), F32),
        compiler_params=params(),
        cost_estimate=pl.CostEstimate(
            flops=2 * sources * dests * batch,
            bytes_accessed=2 * sources * dests,
            transcendentals=0,
        ),
        name="advance",
    )(weights, trans)


def bits_of(count):
    return [1 << k for k in range(count.bit_length() - 1)]


def swapped(value, axis, mask):
    count = lax.axis_size(axis)
    return lax.ppermute(value, axis, [(i, i ^ mask) for i in range(count)])


def summed_all(value, axes):
    for axis in axes:
        for mask in bits_of(lax.axis_size(axis)):
            value = value + swapped(value, axis, mask)
    return value


def merged_rows(stats, rows):
    others = [swapped(stats, "row", mask) for mask in range(1, rows)]
    top = functools.reduce(jnp.maximum, [part[0] for part in others], stats[0])
    totals = [part[1] * jnp.exp(part[0] - top) for part in [stats] + others]
    while len(totals) > 1:
        totals = [first + second for first, second in zip(totals[::2], totals[1::2])]
    return top, totals[0]


def tied(value, others):
    return lax.optimization_barrier((value, *others))[0]


def widths_of(dests):
    unit = block_of(dests, 256)
    count = dests // unit
    first = max(1, count * 5 // 8)
    return [unit * size for size in (first, count - first) if size]


def pair_stages():
    odd = lax.axis_index("row") % 2 == 1

    def apart(value):
        half = value.shape[0] // 2
        low, high = value[:half], value[half:]
        return jnp.where(odd, high, low) + swapped(jnp.where(odd, low, high), "row", 1)

    def across(value):
        return value + swapped(value, "row", 2)

    def together(value):
        other = swapped(value, "row", 1)
        return jnp.concatenate([jnp.where(odd, other, value), jnp.where(odd, value, other)], axis=0)

    return [apart, across, together]


def summed_rows(compute, rows, small, rounds):
    if rows != 4:
        pieces = [part([]) for part in compute]
        small = small(pieces)
        for step in sum(rounds, []):
            small = step(small)
        return [summed_all(part, ("row",)) for part in pieces], small
    stages = pair_stages()
    first = compute[0]([])
    second, moved = lax.optimization_barrier((compute[1]([first]), stages[0](first)))
    small = small([first, second])
    pieces = [moved, second]
    for k in range(1, len(stages) + 1):
        for i in range(2):
            if 0 <= k - i < len(stages):
                pieces[i] = stages[k - i](pieces[i])
        small = tied(small, pieces[1:])
        for step in rounds[k - 1]:
            small = step(small)
        small, *pieces = lax.optimization_barrier((small, *pieces))
    return pieces, small


def root_hops(rows, cols):
    per_row = cols // rows
    if rows == 4:
        lines = {
            0: ([(1, 0), (3, 2)], [(2, 0)]),
            1: ([(0, 1), (3, 2)], [(2, 1)]),
            2: ([(0, 1), (3, 2)], [(1, 2)]),
            3: ([(0, 1), (2, 3)], [(1, 3)]),
        }
    else:
        lines = {
            root: [[(at, root)] for at in range(rows) if at != root] for root in range(rows)
        }
    hops = []
    for hop in range(len(lines[0])):
        perm = [
            (a * cols + col, b * cols + col)
            for col in range(cols)
            for a, b in lines[col // per_row][hop]
        ]
        hops.append(lambda value, perm=perm: lax.ppermute(value, ("row", "col"), perm))
    return hops


def piped(compute, operand, count, hops, small, rounds):
    moving, ready = [], []

    def moved(beside):
        received = [hops[at](value) for value, at in moving if at < len(hops)]
        beside, *received = lax.optimization_barrier((beside(), *received))
        received.reverse()
        return beside, [
            (value + received.pop(), at + 1) if at < len(hops) else (value, at)
            for value, at in moving
        ]

    for k in range(count):
        part, moving = moved(lambda: compute(k, tied(operand, ready) if ready else operand))
        ready = [value for value, at in moving]
        moving.append((part, 0))
    small = small()
    for k in range(len(hops)):

        def beside():
            value = small
            for step in rounds[k]:
                value = step(value)
            return value

        small, moving = moved(beside)
    return [value for value, at in moving], small


def to_sources(block, rows, cols):
    per_row = cols // rows
    row, col = lax.axis_index("row"), lax.axis_index("col")
    group = col // per_row
    relation = group ^ row
    half = block.shape[1] // 2
    first, second = block[:, :half], block[:, half:]

    def sent(value, pairs):
        at = lambda r, mask, m: r * cols + (r ^ mask) * per_row + m
        perm = [
            (at(r, a, m), at(r, b, m)) for r in range(rows) for a, b in pairs for m in range(per_row)
        ]
        return lax.ppermute(value, ("row", "col"), perm)

    near, far = lax.optimization_barrier((sent(first, [(0, 1)]), sent(second, [(0, 2)])))
    first = jnp.where(relation == 0, first, near)
    second = jnp.where(relation == 0, second, far)
    far, near = lax.optimization_barrier(
        (sent(first, [(0, 2), (1, 3)]), sent(second, [(0, 1), (2, 3)]))
    )
    first = jnp.where(relation <= 1, first, far)
    second = jnp.where((relation == 0) | (relation == 2), second, near)
    blocks = jnp.concatenate([first, second], axis=1)
    member = col % per_row
    for mask in bits_of(per_row):
        other = swapped(blocks, "col", mask)
        blocks = jnp.where(
            member & mask == 0,
            jnp.concatenate([blocks, other], axis=1),
            jnp.concatenate([other, blocks], axis=1),
        )
    return blocks


def on_device(src_emb, dst_emb, state_emb, word_emb, start_probs, token_ids):
    rows, cols = lax.axis_size("row"), lax.axis_size("col")
    row = lax.axis_index("row")
    batch, steps = token_ids.shape
    dests = dst_emb.shape[0]
    states = dests * cols

    src_rows = lax.all_gather(src_emb, "col", axis=0, tiled=True)

    vocab = jnp.stack(column_stats(word_emb, state_emb, "vocab_stats"))
    vocab_top, vocab_total = merged_rows(vocab, rows)
    state_norm = vocab_top + jnp.log(vocab_total)

    vocab_rows = word_emb.shape[0]
    flat_ids = token_ids.T.reshape(-1) - row * vocab_rows
    onehot = (flat_ids[:, None] == jnp.arange(vocab_rows, dtype=jnp.int32)[None, :]).astype(BF16)
    picked = jnp.dot(onehot, word_emb, preferred_element_type=F32).astype(BF16)
    token_vecs = summed_all(picked, ("row",))
    scores = logits_of(token_vecs, state_emb)
    emit = jnp.exp(scores - state_norm)

    stats = jnp.stack(column_stats(dst_emb, src_rows, "trans_stats"))
    every = lax.all_gather(stats, "col")
    row_top = jnp.max(every[:, 0], axis=0)
    row_total = jnp.sum(every[:, 1] * jnp.exp(every[:, 0] - row_top[None]), axis=0)

    weights0 = (start_probs.astype(F32) / row_total).astype(BF16)
    top_column = row_top.reshape(-1, 1)
    widths = widths_of(dests)
    starts = [sum(widths[:k]) for k in range(len(widths))]
    here = [slice(at, at + width) for at, width in zip(starts, widths)]

    trans, scales1 = [], []

    def add_rows(value):
        if rows != 4:
            return summed_all(value, ("row",))
        one, two, three = [swapped(value, "row", mask) for mask in (1, 2, 3)]
        return (value + one) + (two + three)


    def add_over(axis, mask):
        return lambda value: value + swapped(value, axis, mask)

    col_rounds = [add_over("col", mask) for mask in bits_of(cols)]

    def first_step(k, weights):
        built, part = build_and_advance(src_rows, dst_emb[here[k]], top_column, weights)
        trans.append(built)
        scales1.append(jnp.sum(part * emit[:batch, here[k]], axis=1))
        return part

    rounds = [col_rounds, [add_rows]] + [[]] * rows
    sums1, scale1 = piped(
        first_step,
        weights0,
        len(widths),
        root_hops(rows, cols),
        lambda: sum(scales1),
        rounds,
    )
    scale1 = scale1 / states
    joint1 = jnp.concatenate(sums1, axis=1) * emit[:batch]
    probs1 = (joint1 / scale1[:, None]).astype(BF16)
    source_probs = to_sources(probs1, rows, cols)
    weights1 = (source_probs.astype(F32) / row_total).astype(BF16)

    sums2, scale2 = summed_rows(
        [
            lambda others, built=built: advance(tied(weights1, others) if others else weights1, built)
            for built in trans
        ],
        rows,
        lambda pieces: sum(
            jnp.sum(part * emit[batch : 2 * batch, at], axis=1) for part, at in zip(pieces, here)
        ),
        [col_rounds, [add_rows], []],
    )
    scale2 = scale2 / states
    final_probs = jnp.concatenate(sums2, axis=1) * emit[batch : 2 * batch] / scale2[:, None]
    log_norm = jnp.log(scale1) + jnp.log(scale2)
    return (final_probs, log_norm)


def solution(mesh):
    in_specs = (
        P(("row", "col"), None),
        P("col", None),
        P("col", None),
        P("row", None),
        P(None, "row"),
        P(),
    )
    out_specs = (P(None, "col"), P())
    return jax.shard_map(
        on_device, mesh=mesh, in_specs=in_specs, out_specs=out_specs, check_vma=False
    )
```

```python
import functools

import jax
import jax.numpy as jnp
from jax import lax
from jax.experimental import pallas as pl
from jax.experimental.pallas import tpu as pltpu
from jax.sharding import PartitionSpec as P

F32 = jnp.float32
BF16 = jnp.bfloat16
NT = (((1,), (1,)), ((), ()))
SPREAD = 60.0
VMEM_LIMIT = 48 * 1024 * 1024
SMALL_LIMIT = 40 * 1024 * 1024


def block_of(count, most):
    return max(size for size in range(16, most + 1, 16) if count % size == 0)


def params(limit=VMEM_LIMIT):
    return pltpu.CompilerParams(vmem_limit_bytes=limit, dimension_semantics=("arbitrary",))


def logits_of(rows, columns):
    return lax.dot_general(rows, columns, NT, preferred_element_type=F32)


def stats_kernel(x_ref, y_ref, top_ref, total_ref, buf0, buf1, *, rows, sub):
    count, columns = x_ref.shape[0], y_ref.shape[0]
    bufs = (buf0, buf1)
    head = min(rows, 256)
    units = [(c, a) for c in range(0, columns, sub) for a in range(0, count, rows)]

    def multiply(unit, buf):
        c, a = unit
        logits = logits_of(x_ref[a : a + rows, :], y_ref[c : c + sub, :])
        buf[...] = logits
        top = jnp.max(logits.reshape(rows // 8, 8, sub), axis=0)
        shift = jnp.max(logits[:head], axis=0, keepdims=True) if a == 0 else None
        return top, shift

    worst = jnp.zeros((1, sub), F32)
    upcoming = multiply(units[0], buf0)
    top = total = shift = None
    for k, (c, a) in enumerate(units):
        unit_top, unit_shift = upcoming
        if a == 0:
            shift, top = unit_shift, unit_top
        else:
            top = jnp.maximum(top, unit_top)
        if k + 1 < len(units):
            upcoming = multiply(units[k + 1], bufs[(k + 1) % 2])
        part = jnp.sum(jnp.exp(bufs[k % 2][...] - shift).reshape(rows // 8, 8, sub), axis=0)
        total = part if a == 0 else total + part
        if a + rows == count:
            total = jnp.sum(total, axis=0, keepdims=True)
            top = jnp.max(top, axis=0, keepdims=True)
            worst = jnp.maximum(worst, top - shift)
            top_ref[:, c : c + sub] = top
            total_ref[:, c : c + sub] = total / jnp.exp(top - shift)

    @pl.when(jnp.max(worst) > SPREAD)
    def again():
        for c in range(0, columns, sub):

            def logits_at(k):
                part = x_ref[pl.ds(pl.multiple_of(k * rows, rows), rows), :]
                return logits_of(part, y_ref[c : c + sub, :])

            def max_step(k, so_far):
                return jnp.maximum(so_far, jnp.max(logits_at(k), axis=0, keepdims=True))

            top = lax.fori_loop(0, count // rows, max_step, jnp.full((1, sub), -jnp.inf, F32))

            def sum_step(k, so_far):
                return so_far + jnp.sum(jnp.exp(logits_at(k) - top), axis=0, keepdims=True)

            total = lax.fori_loop(0, count // rows, sum_step, jnp.zeros((1, sub), F32))
            top_ref[:, c : c + sub] = top
            total_ref[:, c : c + sub] = total


def column_stats(x, y, name):
    count, depth = x.shape
    columns = y.shape[0]
    width = block_of(columns, 1024)
    sub = block_of(width, 256)
    rows = block_of(count, 1024)
    return pl.pallas_call(
        functools.partial(stats_kernel, rows=rows, sub=sub),
        grid=(columns // width,),
        in_specs=[
            pl.BlockSpec((count, depth), lambda i: (0, 0)),
            pl.BlockSpec((width, depth), lambda i: (i, 0)),
        ],
        out_specs=[pl.BlockSpec((1, width), lambda i: (0, i))] * 2,
        out_shape=[jax.ShapeDtypeStruct((1, columns), F32)] * 2,
        scratch_shapes=[pltpu.VMEM((rows, sub), F32)] * 2,
        compiler_params=params(),
        cost_estimate=pl.CostEstimate(
            flops=2 * count * columns * depth,
            bytes_accessed=2 * depth * (count + columns),
            transcendentals=count * columns,
        ),
        name=name,
    )(x, y)


def trans_kernel(src_ref, dst_ref, top_ref, weight_ref, trans_ref, out_ref, buf0, buf1, *, cols):
    count = dst_ref.shape[0] // cols
    bufs = (buf0, buf1)

    @pl.when(pl.program_id(0) == 0)
    def _():
        out_ref[...] = jnp.zeros_like(out_ref)

    def multiply(k):
        bufs[k % 2][...] = logits_of(src_ref[...], dst_ref[k * cols : (k + 1) * cols, :])

    def advance(k):
        here = slice(k * cols, (k + 1) * cols)
        out_ref[:, here] += jnp.dot(
            weight_ref[...], trans_ref[:, here], preferred_element_type=F32
        )

    multiply(0)
    for k in range(count):
        if k + 1 < count:
            multiply(k + 1)
        shifted = jnp.exp(bufs[k % 2][...] - top_ref[...])
        trans_ref[:, k * cols : (k + 1) * cols] = shifted.astype(BF16)
        if k > 0:
            advance(k - 1)
    advance(count - 1)


def build_and_advance(src, dst, top, weights, limit):
    sources, depth = src.shape
    dests = dst.shape[0]
    batch = weights.shape[0]
    rows = block_of(sources, 1024)
    cols = block_of(dests, 256)
    return pl.pallas_call(
        functools.partial(trans_kernel, cols=cols),
        grid=(sources // rows,),
        in_specs=[
            pl.BlockSpec((rows, depth), lambda i: (i, 0)),
            pl.BlockSpec((dests, depth), lambda i: (0, 0)),
            pl.BlockSpec((rows, 1), lambda i: (i, 0)),
            pl.BlockSpec((batch, rows), lambda i: (0, i)),
        ],
        out_specs=[
            pl.BlockSpec((rows, dests), lambda i: (i, 0)),
            pl.BlockSpec((batch, dests), lambda i: (0, 0)),
        ],
        out_shape=[
            jax.ShapeDtypeStruct((sources, dests), BF16),
            jax.ShapeDtypeStruct((batch, dests), F32),
        ],
        scratch_shapes=[pltpu.VMEM((rows, cols), F32)] * 2,
        compiler_params=params(limit),
        cost_estimate=pl.CostEstimate(
            flops=2 * sources * dests * (depth + batch),
            bytes_accessed=2 * sources * dests,
            transcendentals=sources * dests,
        ),
        name="build_trans",
    )(src, dst, top, weights)


def advance_kernel(weight_ref, trans_ref, out_ref):
    @pl.when(pl.program_id(0) == 0)
    def _():
        out_ref[...] = jnp.zeros_like(out_ref)

    out_ref[...] += jnp.dot(weight_ref[...], trans_ref[...], preferred_element_type=F32)


def advance(weights, trans):
    sources, dests = trans.shape
    batch = weights.shape[0]
    rows = block_of(sources, 2048)
    return pl.pallas_call(
        advance_kernel,
        grid=(sources // rows,),
        in_specs=[
            pl.BlockSpec((batch, rows), lambda i: (0, i)),
            pl.BlockSpec((rows, dests), lambda i: (i, 0)),
        ],
        out_specs=pl.BlockSpec((batch, dests), lambda i: (0, 0)),
        out_shape=jax.ShapeDtypeStruct((batch, dests), F32),
        compiler_params=params(),
        cost_estimate=pl.CostEstimate(
            flops=2 * sources * dests * batch,
            bytes_accessed=2 * sources * dests,
            transcendentals=0,
        ),
        name="advance",
    )(weights, trans)


def bits_of(count):
    return [1 << k for k in range(count.bit_length() - 1)]


def swapped(value, axis, mask):
    count = lax.axis_size(axis)
    return lax.ppermute(value, axis, [(i, i ^ mask) for i in range(count)])


def summed_all(value, axes):
    for axis in axes:
        for mask in bits_of(lax.axis_size(axis)):
            value = value + swapped(value, axis, mask)
    return value


def merged_rows(stats, rows):
    others = [swapped(stats, "row", mask) for mask in range(1, rows)]
    top = functools.reduce(jnp.maximum, [part[0] for part in others], stats[0])
    totals = [part[1] * jnp.exp(part[0] - top) for part in [stats] + others]
    while len(totals) > 1:
        totals = [first + second for first, second in zip(totals[::2], totals[1::2])]
    return top, totals[0]


def tied(value, others):
    return lax.optimization_barrier((value, *others))[0]


def widths_of(dests):
    unit = block_of(dests, 256)
    count = dests // unit
    first = max(1, count * 5 // 8)
    return [unit * size for size in (first, count - first) if size]


def pair_stages():
    odd = lax.axis_index("row") % 2 == 1

    def apart(value):
        half = value.shape[0] // 2
        low, high = value[:half], value[half:]
        return jnp.where(odd, high, low) + swapped(jnp.where(odd, low, high), "row", 1)

    def across(value):
        return value + swapped(value, "row", 2)

    def together(value):
        other = swapped(value, "row", 1)
        return jnp.concatenate([jnp.where(odd, other, value), jnp.where(odd, value, other)], axis=0)

    return [apart, across, together]


def summed_rows(compute, rows, small, rounds):
    if rows != 4:
        pieces = [part([]) for part in compute]
        small = small(pieces)
        for step in sum(rounds, []):
            small = step(small)
        return [summed_all(part, ("row",)) for part in pieces], small
    stages = pair_stages()
    first = compute[0]([])
    second, moved = lax.optimization_barrier((compute[1]([first]), stages[0](first)))
    small = small([first, second])
    pieces = [moved, second]
    for k in range(1, len(stages) + 1):
        for i in range(2):
            if 0 <= k - i < len(stages):
                pieces[i] = stages[k - i](pieces[i])
        if k == 1:
            small = tied(small, pieces[1:])
        for step in rounds[k - 1]:
            small = step(small)
        small, *pieces = lax.optimization_barrier((small, *pieces))
    return pieces, small


def root_hops(rows, cols):
    per_row = cols // rows
    if rows == 4:
        lines = {
            0: ([(1, 0), (3, 2)], [(2, 0)]),
            1: ([(0, 1), (3, 2)], [(2, 1)]),
            2: ([(0, 1), (3, 2)], [(1, 2)]),
            3: ([(0, 1), (2, 3)], [(1, 3)]),
        }
    else:
        lines = {
            root: [[(at, root)] for at in range(rows) if at != root] for root in range(rows)
        }
    hops = []
    for hop in range(len(lines[0])):
        perm = [
            (a * cols + col, b * cols + col)
            for col in range(cols)
            for a, b in lines[col // per_row][hop]
        ]
        hops.append(lambda value, perm=perm: lax.ppermute(value, ("row", "col"), perm))
    return hops


def piped(compute, operand, count, hops, small, rounds):
    moving, ready = [], []

    def moved(beside):
        received = [hops[at](value) for value, at in moving if at < len(hops)]
        beside, *received = lax.optimization_barrier((beside(), *received))
        received.reverse()
        return beside, [
            (value + received.pop(), at + 1) if at < len(hops) else (value, at)
            for value, at in moving
        ]

    for k in range(count):
        part, moving = moved(lambda: compute(k, tied(operand, ready) if ready else operand))
        ready = [value for value, at in moving]
        moving.append((part, 0))
    small = small()
    for k in range(len(hops)):

        def beside():
            value = small
            for step in rounds[k]:
                value = step(value)
            return value

        small, moving = moved(beside)
    return [value for value, at in moving], small


def to_sources(block, rows, cols):
    per_row = cols // rows
    row, col = lax.axis_index("row"), lax.axis_index("col")
    group = col // per_row
    relation = group ^ row
    half = block.shape[1] // 2
    first, second = block[:, :half], block[:, half:]

    def sent(value, pairs):
        at = lambda r, mask, m: r * cols + (r ^ mask) * per_row + m
        perm = [
            (at(r, a, m), at(r, b, m)) for r in range(rows) for a, b in pairs for m in range(per_row)
        ]
        return lax.ppermute(value, ("row", "col"), perm)

    near, far = lax.optimization_barrier((sent(first, [(0, 1)]), sent(second, [(0, 2)])))
    first = jnp.where(relation == 0, first, near)
    second = jnp.where(relation == 0, second, far)
    far, near = lax.optimization_barrier(
        (sent(first, [(0, 2), (1, 3)]), sent(second, [(0, 1), (2, 3)]))
    )
    first = jnp.where(relation <= 1, first, far)
    second = jnp.where((relation == 0) | (relation == 2), second, near)
    blocks = jnp.concatenate([first, second], axis=1)
    member = col % per_row
    for mask in bits_of(per_row):
        other = swapped(blocks, "col", mask)
        blocks = jnp.where(
            member & mask == 0,
            jnp.concatenate([blocks, other], axis=1),
            jnp.concatenate([other, blocks], axis=1),
        )
    return blocks


def on_device(src_emb, dst_emb, state_emb, word_emb, start_probs, token_ids):
    rows, cols = lax.axis_size("row"), lax.axis_size("col")
    row = lax.axis_index("row")
    batch, steps = token_ids.shape
    dests = dst_emb.shape[0]
    states = dests * cols

    src_rows = lax.all_gather(src_emb, "col", axis=0, tiled=True)

    vocab = jnp.stack(column_stats(word_emb, state_emb, "vocab_stats"))
    vocab_top, vocab_total = merged_rows(vocab, rows)
    state_norm = vocab_top + jnp.log(vocab_total)

    vocab_rows = word_emb.shape[0]
    flat_ids = token_ids.T.reshape(-1) - row * vocab_rows
    onehot = (flat_ids[:, None] == jnp.arange(vocab_rows, dtype=jnp.int32)[None, :]).astype(BF16)
    picked = jnp.dot(onehot, word_emb, preferred_element_type=F32).astype(BF16)
    token_vecs = summed_all(picked, ("row",))
    scores = logits_of(token_vecs, state_emb)
    emit = jnp.exp(scores - state_norm)

    stats = jnp.stack(column_stats(dst_emb, src_rows, "trans_stats"))
    every = lax.all_gather(stats, "col")
    row_top = jnp.max(every[:, 0], axis=0)
    row_total = jnp.sum(every[:, 1] * jnp.exp(every[:, 0] - row_top[None]), axis=0)

    weights0 = (start_probs.astype(F32) / row_total).astype(BF16)
    top_column = row_top.reshape(-1, 1)
    widths = widths_of(dests)
    starts = [sum(widths[:k]) for k in range(len(widths))]
    here = [slice(at, at + width) for at, width in zip(starts, widths)]

    trans, scales1 = [], []

    def add_rows(value):
        if rows != 4:
            return summed_all(value, ("row",))
        one, two, three = [swapped(value, "row", mask) for mask in (1, 2, 3)]
        return (value + one) + (two + three)


    def add_over(axis, mask):
        return lambda value: value + swapped(value, axis, mask)

    col_rounds = [add_over("col", mask) for mask in bits_of(cols)]

    def first_step(k, weights):
        built, part = build_and_advance(
            src_rows, dst_emb[here[k]], top_column, weights, VMEM_LIMIT if k == 0 else SMALL_LIMIT
        )
        trans.append(built)
        scales1.append(jnp.sum(part * emit[:batch, here[k]], axis=1))
        return part

    rounds = [col_rounds, [add_rows]] + [[]] * rows
    sums1, scale1 = piped(
        first_step,
        weights0,
        len(widths),
        root_hops(rows, cols),
        lambda: sum(scales1),
        rounds,
    )
    scale1 = scale1 / states
    joint1 = jnp.concatenate(sums1, axis=1) * emit[:batch]
    probs1 = (joint1 / scale1[:, None]).astype(BF16)
    source_probs = to_sources(probs1, rows, cols)
    weights1 = (source_probs.astype(F32) / row_total).astype(BF16)

    sums2, scale2 = summed_rows(
        [
            lambda others, built=built: advance(tied(weights1, others) if others else weights1, built)
            for built in trans
        ],
        rows,
        lambda pieces: sum(
            jnp.sum(part * emit[batch : 2 * batch, at], axis=1) for part, at in zip(pieces, here)
        ),
        [col_rounds, [add_rows], []],
    )
    scale2 = scale2 / states
    final_probs = jnp.concatenate(sums2, axis=1) * emit[batch : 2 * batch] / scale2[:, None]
    log_norm = jnp.log(scale1) + jnp.log(scale2)
    return (final_probs, log_norm)


def solution(mesh):
    in_specs = (
        P(("row", "col"), None),
        P("col", None),
        P("col", None),
        P("row", None),
        P(None, "row"),
        P(),
    )
    out_specs = (P(None, "col"), P())
    return jax.shard_map(
        on_device, mesh=mesh, in_specs=in_specs, out_specs=out_specs, check_vma=False
    )
```
